32 devices in a mesh: groups: 2 (over y), feat: 4 (over z), layer: 4 (over x, core).
Axes of the slice: x: 2, y: 2, z: 4, core: 2. Of those that a mesh axis runs over, the one named last changes fastest.
Arguments:
- inputs: bfloat16 [2, 1024, 2048], P(None, ('groups', 'feat')), parts along dimension 1, may hold values from -6 to 6
- targets: bfloat16 [1024, 2, 2048], P(('groups', 'feat')), parts along dimension 0, may hold values from -6 to 6
- block_mask: int32 [2, 256, 1024], P(None, 'feat', 'groups'), parts along dimension 2, may hold values 0 or 1
- enc_weight: bfloat16 [2, 32768, 2048], P(None, ('feat', 'layer')), may hold values from -0.125 to 0.125
- enc_bias: float32 [2, 32768], P(None, ('feat', 'layer')), may hold values from -3 to 3
- threshold: float32 [2, 32768], P(None, ('feat', 'layer')), may hold values from 0.3 to 1.2
- dec_weight: bfloat16 [3, 32768, 2048], P(None, ('feat', 'layer')), may hold values from -0.09375 to 0.09375
Outputs:
- grad_enc: bfloat16 [4, 32768, 2048], P('groups', ('feat', 'layer')), parts along dimension 0
- grad_bias: float32 [4, 32768], P('groups', ('feat', 'layer')), parts along dimension 0
- grad_threshold: float32 [4, 32768], P('groups', ('feat', 'layer')), parts along dimension 0
- grad_dec: bfloat16 [6, 32768, 2048], P('groups', ('feat', 'layer')), parts along dimension 0
The draws below stay inside these ranges and needn't reach their ends.
There are 2 independent parts, one for each index of `groups`. The reference program is written for one: setup_inputs(seed, part) draws one part's arguments, and reference() takes and returns one part's arrays. A program takes and returns all parts, laid end to end along the dimension named above; an argument that names none is the same for every part. Nothing has to cross between parts.
All inputs are finite; a program needn't handle non-finite values. No bound on the sum of `block_mask` on one device may be relied on, other than what follows from the above.
Results may differ from the reference program's by a relative error of at most 0.015.
Values may be sent and summed in bfloat16 or wider, within the bound.
A program may use at most 256 MiB of HBM per device.

```python
import math
import jax
import jax.numpy as jnp
from jax import lax

D = 2048
F = 32768
LAYERS = 2
BLOCK = 128
ROWS = 512
PAIRS = 3
BLOCKS = 256
N_FEAT = 4
N_LAYER = 4


def set_ends(array, stream_key, smallest, high):
    shape = array.shape
    place = [jax.random.randint(jax.random.fold_in(stream_key, axis), (), 0, shape[axis]) for axis in range(len(shape))]
    array = array.at[tuple(place)].set(smallest)
    longest = shape.index(max(shape))
    place[longest] = (place[longest] + 1) % shape[longest]
    return array.at[tuple(place)].set(high)


def shard_levels(stream_key, shape, split, least, largest):
    gain, own = 1.0, jax.random.fold_in(stream_key, 6)
    for position, parts in split:
        draws = jnp.exp(jax.random.uniform(jax.random.fold_in(own, position), (parts,), jnp.float32, least / len(split), largest / len(split)))
        gain = gain * jnp.repeat(draws, shape[position] // parts).reshape([-1 if axis == position else 1 for axis in range(len(shape))])
    return gain


def bell_draw(own_key, dims, deviation, bound, shards=(), kind=jnp.bfloat16):
    result = jax.random.normal(own_key, dims, jnp.float32) * deviation
    if len(shards) > 0:
        result = shard_levels(own_key, dims, shards, -0.22, 0.18) * result
    return jnp.clip(result, min=-bound, max=bound).astype(kind)


def setup_inputs(seed: int = 0, part: int = 0) -> dict:
    seeds = jax.random.split(jax.random.key(seed), 8)
    part_keys = jax.random.split(jax.random.fold_in(seeds[7], part), 8)
    inputs = bell_draw(part_keys[0], (LAYERS, ROWS, D), 1.0, 6.0, ((1, 4),))
    targets = bell_draw(part_keys[1], (ROWS, LAYERS, D), 1.0, 6.0, ((0, 4),))
    block_mask = set_ends((jax.random.randint(part_keys[2], (LAYERS, BLOCKS, ROWS), 0, 3) < 1).astype(jnp.int32), jax.random.fold_in(part_keys[2], 1), 0, 1)
    enc_weight = bell_draw(seeds[3], (LAYERS, F, D), D ** -0.5, 0.125, ((1, 16),))
    enc_bias = bell_draw(seeds[4], (LAYERS, F), 0.5, 3.0, ((1, 16),), jnp.float32)
    threshold = jnp.clip(jnp.exp(math.log(1.2) - 1.3862944 * jax.random.uniform(seeds[5], (LAYERS, F), jnp.float32) ** shard_levels(seeds[5], (LAYERS, F), ((1, 16),), -0.2, 0.2)), 0.3, 1.2)
    dec_weight = bell_draw(seeds[6], (PAIRS, F, D), (F // 8) ** -0.5, 0.09375, ((1, 16),))
    return dict(inputs=inputs, targets=targets, block_mask=block_mask, enc_weight=enc_weight, enc_bias=enc_bias, threshold=threshold, dec_weight=dec_weight)


BAND = 0.2


def pair_list():
    return [(source, target) for source in range(LAYERS) for target in range(source, LAYERS)]


def reference(inputs, targets, block_mask, enc_weight, enc_bias, threshold, dec_weight):
    pairs = pair_list()
    preact = jnp.einsum("lrd,lfd->lrf", inputs.astype(jnp.float32), enc_weight.astype(jnp.float32)) + enc_bias[:, None, :]
    gates = jnp.transpose(jnp.repeat(block_mask, BLOCK, axis=1), (0, 2, 1)).astype(jnp.float32)
    squash = jax.nn.sigmoid((preact - threshold[:, None, :]) / BAND)
    hidden = (gates * preact * squash).astype(jnp.bfloat16)
    group_count = N_FEAT * N_LAYER
    width = F // group_count

    def add_group(summed, group):
        first = (group * width).astype(jnp.int32)
        local = lax.dynamic_slice_in_dim(hidden, first, width, 2)
        columns = []
        for target in range(LAYERS):
            total = jnp.zeros((ROWS, D), jnp.float32)
            for index, (source, goal) in enumerate(pairs):
                if goal == target:
                    weights = lax.dynamic_slice_in_dim(dec_weight[index], first, width, 0)
                    total = total + jnp.dot(local[source], weights, preferred_element_type=jnp.float32)
            columns.append(total)
        partial_value = lax.optimization_barrier(jnp.stack(columns, 1).astype(jnp.bfloat16))
        return summed + partial_value.astype(jnp.float32), None

    decoded, unused = lax.scan(add_group, jnp.zeros((ROWS, LAYERS, D), jnp.float32), jnp.arange(group_count, dtype=jnp.int32))
    error = (decoded - targets.astype(jnp.float32)).astype(jnp.bfloat16)
    back_list = [jnp.zeros((ROWS, F), jnp.float32) for source in range(LAYERS)]
    dec_grads = []
    for index, (source, goal) in enumerate(pairs):
        back_list[source] = back_list[source] + lax.dot_general(error[:, goal], dec_weight[index], (((1,), (1,)), ((), ())), preferred_element_type=jnp.float32)
        dec_grads.append(lax.dot_general(hidden[source], error[:, goal], (((0,), (0,)), ((), ())), preferred_element_type=jnp.float32).astype(jnp.bfloat16))
    back_grad = jnp.stack(back_list, 0)
    bend = squash * (1.0 - squash) / BAND
    slope = gates * (squash + preact * bend)
    grad_pre = back_grad * slope
    grad_bias = jnp.sum(grad_pre, axis=1)
    grad_threshold = -jnp.sum(back_grad * gates * preact * bend, axis=1)
    grad_rounded = grad_pre.astype(jnp.bfloat16)
    grad_enc = jnp.einsum("lrf,lrd->lfd", grad_rounded.astype(jnp.float32), inputs.astype(jnp.float32)).astype(jnp.bfloat16)
    return grad_enc, grad_bias, grad_threshold, jnp.stack(dec_grads, 0)
```

```python
import functools

import jax
import jax.numpy as jnp
from jax import lax
from jax.experimental import pallas as pl
from jax.experimental.pallas import tpu as pltpu
from jax.sharding import PartitionSpec as P

BLOCK = 128
BAND = 0.2
LANES = 128
MESH = pl.DeviceIdType.MESH
MIB = 1 << 20


def bits(index, stages):
    return [(index // (1 << j)) % 2 for j in range(stages)]


def bases(index_bits, count):
    out = [0]
    for j, bit in enumerate(index_bits):
        out.append(out[-1] + bit * (count >> (j + 1)))
    return out


def partners(index, index_bits):
    return [index + (1 - 2 * bit) * (1 << j) for j, bit in enumerate(index_bits)]


def greet(n_feat, feat, mates):
    barrier = pltpu.get_barrier_semaphore()
    for mate in mates:
        pl.semaphore_signal(barrier, inc=1, device_id={"layer": mate}, device_id_type=MESH)

    def one(o, carry):
        pl.semaphore_signal(
            barrier, inc=1, device_id={"feat": (feat + o) % n_feat}, device_id_type=MESH
        )
        return carry

    lax.fori_loop(1, n_feat, one, 0)
    pl.semaphore_wait(barrier, len(mates) + n_feat - 1)


def remote(src, dst, send, recv, where):
    return pltpu.make_async_remote_copy(
        src_ref=src, dst_ref=dst, send_sem=send, recv_sem=recv, device_id=where, device_id_type=MESH
    )


def gather_kernel(n_feat, n_layer, x_ref, out_ref, z_send, z_recv, l_send, l_recv, own_sem):
    feat, place = lax.axis_index("feat"), lax.axis_index("layer")
    stages = n_layer.bit_length() - 1
    rows = x_ref.shape[1]
    width = x_ref.shape[2] // n_layer
    place_bits = bits(place, stages)
    base = bases(place_bits, n_layer)
    mates = partners(place, place_bits)
    greet(n_feat, feat, mates)

    def at(ref, source, first, count):
        return ref.at[
            :,
            pl.ds(pl.multiple_of(source * rows, rows), rows),
            pl.ds(pl.multiple_of(first * width, width), count * width),
        ]

    def z_copy(o):
        mine = at(out_ref, feat, base[stages], 1)
        src = x_ref.at[:, :, pl.ds(pl.multiple_of(base[stages] * width, width), width)]
        return remote(src, mine, z_send.at[o - 1], z_recv.at[o - 1], {"feat": (feat + o) % n_feat})

    def l_copy(j, o):
        part = at(out_ref, (feat + n_feat - o) % n_feat, base[j + 1], n_layer >> (j + 1))
        return remote(part, part, l_send.at[j, o - 1], l_recv.at[j, o - 1], {"layer": mates[j]})

    def start_z(o, carry):
        z_copy(o).start()
        return carry

    lax.fori_loop(1, n_feat, start_z, 0)
    own = pltpu.make_async_copy(
        x_ref, out_ref.at[:, pl.ds(pl.multiple_of(feat * rows, rows), rows), :], own_sem
    )
    own.start()
    for j in reversed(range(-1, stages)):

        def hop(o, carry, j=j):
            if j == stages - 1:
                z_copy(o).wait_recv()
            else:
                l_copy(j + 1, o).wait_recv()
            if j >= 0:
                l_copy(j, o).start()
            return carry

        lax.fori_loop(1, n_feat, hop, 0)

    def drain(o, carry):
        z_copy(o).wait_send()
        for j in range(stages):
            l_copy(j, o).wait_send()
        return carry

    lax.fori_loop(1, n_feat, drain, 0)
    own.wait()


def gather(inputs, n_feat, n_layer):
    layers, rows, width = inputs.shape
    stages = n_layer.bit_length() - 1
    return pl.pallas_call(
        functools.partial(gather_kernel, n_feat, n_layer),
        out_shape=jax.ShapeDtypeStruct((layers, rows * n_feat, width), inputs.dtype),
        in_specs=[pl.BlockSpec(memory_space=pltpu.VMEM)],
        out_specs=pl.BlockSpec(memory_space=pltpu.VMEM),
        scratch_shapes=[
            pltpu.SemaphoreType.DMA((n_feat - 1,)),
            pltpu.SemaphoreType.DMA((n_feat - 1,)),
            pltpu.SemaphoreType.DMA((stages, n_feat - 1)),
            pltpu.SemaphoreType.DMA((stages, n_feat - 1)),
            pltpu.SemaphoreType.DMA,
        ],
        compiler_params=pltpu.CompilerParams(
            collective_id=0, has_side_effects=True, vmem_limit_bytes=16 * MIB
        ),
        name="gather_rows",
    )(inputs)


def gate_tile(mask_ref, values):
    mask = mask_ref[0, 0]
    shape = (mask.shape[0], BLOCK, values.shape[1])
    return jnp.broadcast_to(mask[:, None, :], shape).reshape(values.shape)


def encode_kernel(x_ref, w_ref, bias_ref, thr_ref, mask_ref, pre_ref, turned_ref, hidden_ref):
    pre = (
        lax.dot_general(
            w_ref[0], x_ref[0], (((1,), (1,)), ((), ())), preferred_element_type=jnp.float32
        )
        + bias_ref[0]
    )
    squash = jax.nn.sigmoid((pre - thr_ref[0]) / BAND)
    hidden = (gate_tile(mask_ref, pre) * pre * squash).astype(jnp.bfloat16)
    pre_ref[0] = pre
    turned_ref[0] = hidden
    hidden_ref[0] = hidden.T


def encode(whole, enc_weight, bias, thr, mask):
    layers, count, width = whole.shape
    features = enc_weight.shape[1]
    tile = min(512, features)
    column = pl.BlockSpec((1, tile, 1), lambda l, t: (l, t, 0))
    turned = pl.BlockSpec((1, tile, count), lambda l, t: (l, t, 0))
    return pl.pallas_call(
        encode_kernel,
        grid=(layers, features // tile),
        out_shape=(
            jax.ShapeDtypeStruct((layers, features, count), jnp.float32),
            jax.ShapeDtypeStruct((layers, features, count), jnp.bfloat16),
            jax.ShapeDtypeStruct((layers, count, features), jnp.bfloat16),
        ),
        in_specs=[
            pl.BlockSpec((1, count, width), lambda l, t: (l, 0, 0)),
            pl.BlockSpec((1, tile, width), lambda l, t: (l, t, 0)),
            column,
            column,
            pl.BlockSpec((1, 1, tile // BLOCK, count), lambda l, t: (l, t, 0, 0)),
        ],
        out_specs=(turned, turned, pl.BlockSpec((1, count, tile), lambda l, t: (l, 0, t))),
        compiler_params=pltpu.CompilerParams(vmem_limit_bytes=40 * MIB),
        name="encode",
    )(whole, enc_weight, bias, thr, mask)


def exchange_kernel(
    n_feat, n_layer, hidden_ref, w_hbm, tgt_ref, err_ref, back_ref,
    wbuf, dec, z_got, w_sem, z_send, z_recv, g_send, g_recv, r_send, r_recv, a_send, a_recv, *got,
):
    feat, place = lax.axis_index("feat"), lax.axis_index("layer")
    stages = n_layer.bit_length() - 1
    layers, count, features = hidden_ref.shape
    rows = count // n_feat
    chunks = dec.shape[0]
    cols = n_layer * LANES
    splits = chunks // layers
    pairs = wbuf.shape[0]
    place_bits = bits(place, stages)
    base = bases(place_bits, n_layer)
    mates = partners(place, place_bits)
    mine = base[stages]
    held = [n_layer >> (j + 1) for j in range(stages)]

    def load(p, n):
        part = w_hbm.at[p, :, pl.ds(n * cols, cols)]
        return pltpu.make_async_copy(part, wbuf.at[p, n], w_sem.at[p, n])

    for n in range(splits):
        for p in range(pairs):
            load(p, n).start()
    greet(n_feat, feat, mates)

    tile = min(512, features)

    @pl.loop(0, layers * (features // tile))
    def _(i):
        l, t = i // (features // tile), i % (features // tile)
        back_ref[l, pl.ds(pl.multiple_of(t * tile, tile), tile), :] = jnp.zeros(
            (tile, count), jnp.float32
        )

    def reduce_copy(j, k):
        away = base[j] + (1 - place_bits[j]) * held[j]
        return remote(
            dec.at[k, pl.ds(away, held[j])], got[j].at[k],
            r_send.at[j, k], r_recv.at[j, k], {"layer": mates[j]},
        )

    def spread_copy(j, k):
        part = err_ref.at[k, pl.ds(base[j + 1], held[j])]
        return remote(part, part, a_send.at[j, k], a_recv.at[j, k], {"layer": mates[j]})

    def own_rows(which):
        return pl.ds(pl.multiple_of(which * rows, rows), rows)

    def all_bytes(k, sem):
        return pltpu.make_async_copy(z_got.at[k], z_got.at[k], sem)

    def decode(k):
        m, n = k % layers, k // layers
        wide = min(2, n_layer)

        def run(sources):
            for p in sources:
                load(p, n).wait()

            @pl.loop(0, n_layer // wide)
            def _(c):
                lanes = pl.ds(pl.multiple_of(c * wide * LANES, wide * LANES), wide * LANES)
                total = None
                for p, l in sources.items():
                    term = jnp.dot(
                        hidden_ref[l], wbuf[p, n, :, lanes], preferred_element_type=jnp.float32
                    )
                    total = term if total is None else total + term
                total = total.astype(jnp.bfloat16)
                for i in range(wide):
                    dec[k, c * wide + i] = total[:, i * LANES : (i + 1) * LANES]

        pl.when(m == 0)(lambda: run({0: 0}))
        pl.when(m == 1)(lambda: run({1: 0, 2: 1}))
        reduce_copy(0, k).start()

    def fold(j, k):
        reduce_copy(j, k).wait_recv()
        part = pl.ds(base[j + 1], held[j])
        total = dec[k, part].astype(jnp.float32) + got[j][k].astype(jnp.float32)
        dec[k, part] = total.astype(jnp.bfloat16)
        if j + 1 < stages:
            reduce_copy(j + 1, k).start()
        else:

            def send(o, carry):
                there = (feat + o) % n_feat
                remote(
                    dec.at[k, mine, own_rows(there)], z_got.at[k, o - 1],
                    z_send.at[k], z_recv.at[k], {"feat": there},
                ).start()
                return carry

            lax.fori_loop(1, n_feat, send, 0)

    def finish(k):
        all_bytes(k, z_recv.at[k]).wait()
        m, n = k % layers, k // layers
        total = dec[k, mine, own_rows(feat)].astype(jnp.float32)
        total = total + jnp.sum(z_got[k].astype(jnp.float32), axis=0)
        error = total - tgt_ref[m, n].astype(jnp.float32)
        part = err_ref.at[k, mine, own_rows(feat)]
        part[...] = error.astype(jnp.bfloat16)

        def send(o, carry):
            there = (feat + o) % n_feat
            remote(part, part, g_send.at[k], g_recv.at[k], {"feat": there}).start()
            return carry

        lax.fori_loop(1, n_feat, send, 0)

    def spread(j, k):
        if j == stages - 1:
            all_bytes(k, g_recv.at[k]).wait()
        else:
            spread_copy(j + 1, k).wait_recv()
        spread_copy(j, k).start()

    def pull(k):
        spread_copy(0, k).wait_recv()
        m, n = k % layers, k // layers

        def run(sources):
            error = jnp.concatenate([err_ref[k, b] for b in range(n_layer)], axis=1)
            for p, l in sources.items():

                @pl.loop(0, features // tile)
                def _(t, p=p, l=l):
                    part = pl.ds(pl.multiple_of(t * tile, tile), tile)
                    back_ref[l, part, :] += lax.dot_general(
                        wbuf[p, n, part, :], error, (((1,), (1,)), ((), ())),
                        preferred_element_type=jnp.float32,
                    )

        pl.when(m == 0)(lambda: run({0: 0}))
        pl.when(m == 1)(lambda: run({1: 0, 2: 1}))

    steps = [decode]
    steps += [functools.partial(fold, j) for j in range(stages)]
    steps += [finish]
    steps += [functools.partial(spread, j) for j in reversed(range(stages))]
    steps += [pull]

    @pl.loop(0, chunks + len(steps) - 1)
    def _(s):
        for late in reversed(range(1, len(steps) - 1)):
            k = s - late
            pl.when((k >= 0) & (k < chunks))(functools.partial(steps[late], k))
        pl.when(s < chunks)(functools.partial(decode, s))
        k = s - (len(steps) - 1)
        pl.when(k >= 0)(functools.partial(pull, k))

    @pl.loop(0, chunks)
    def _(k):
        all_bytes(k, z_send.at[k]).wait()
        all_bytes(k, g_send.at[k]).wait()
        for j in range(stages):
            reduce_copy(j, k).wait_send()
            spread_copy(j, k).wait_send()


def exchange(hidden, dec_weight, tgt, n_feat, n_layer):
    layers, count, features = hidden.shape
    pairs, _, width = dec_weight.shape
    stages = n_layer.bit_length() - 1
    splits = width // (n_layer * LANES)
    chunks = splits * layers
    rows = count // n_feat
    dma = pltpu.SemaphoreType.DMA
    vmem = pl.BlockSpec(memory_space=pltpu.VMEM)
    return pl.pallas_call(
        functools.partial(exchange_kernel, n_feat, n_layer),
        out_shape=(
            jax.ShapeDtypeStruct((chunks, n_layer, count, LANES), jnp.bfloat16),
            jax.ShapeDtypeStruct((layers, features, count), jnp.float32),
        ),
        in_specs=[vmem, pl.BlockSpec(memory_space=pl.ANY), vmem],
        out_specs=(vmem, vmem),
        scratch_shapes=[
            pltpu.VMEM((pairs, splits, features, n_layer * LANES), jnp.bfloat16),
            pltpu.VMEM((chunks, n_layer, count, LANES), jnp.bfloat16),
            pltpu.VMEM((chunks, n_feat - 1, rows, LANES), jnp.bfloat16),
            dma((pairs, splits)),
            dma((chunks,)),
            dma((chunks,)),
            dma((chunks,)),
            dma((chunks,)),
            dma((stages, chunks)),
            dma((stages, chunks)),
            dma((stages, chunks)),
            dma((stages, chunks)),
        ]
        + [
            pltpu.VMEM((chunks, n_layer >> (j + 1), count, LANES), jnp.bfloat16)
            for j in range(stages)
        ],
        compiler_params=pltpu.CompilerParams(
            collective_id=1, has_side_effects=True, vmem_limit_bytes=60 * MIB
        ),
        name="decode_exchange",
    )(hidden, dec_weight, tgt)


def grad_dec_kernel(layers, turned_ref, err_ref, out_ref):
    goal = (pl.program_id(0) + 1) // 2
    n_layer = err_ref.shape[1]
    cols = n_layer * LANES
    for n in range(err_ref.shape[0] // layers):
        error = jnp.concatenate([err_ref[n * layers + goal, b] for b in range(n_layer)], axis=1)
        out_ref[0, :, n * cols : (n + 1) * cols] = jnp.dot(
            turned_ref[0], error, preferred_element_type=jnp.float32
        ).astype(jnp.bfloat16)


def grad_dec(turned, err, pairs, width):
    layers, features, count = turned.shape
    tile = min(512, features)
    return pl.pallas_call(
        functools.partial(grad_dec_kernel, layers),
        grid=(pairs, features // tile),
        out_shape=jax.ShapeDtypeStruct((pairs, features, width), jnp.bfloat16),
        in_specs=[
            pl.BlockSpec((1, tile, count), lambda p, t: (p // 2, t, 0)),
            pl.BlockSpec(err.shape, lambda p, t: (0, 0, 0, 0)),
        ],
        out_specs=pl.BlockSpec((1, tile, width), lambda p, t: (p, t, 0)),
        compiler_params=pltpu.CompilerParams(vmem_limit_bytes=40 * MIB),
        name="grad_dec",
    )(turned, err)


def grad_enc_kernel(back_ref, pre_ref, thr_ref, mask_ref, x_ref, out_ref, bias_ref, gthr_ref):
    pre = pre_ref[0]
    back = back_ref[0]
    squash = jax.nn.sigmoid((pre - thr_ref[0]) / BAND)
    bend = squash * (1.0 - squash) / BAND
    gated = back * gate_tile(mask_ref, pre)
    curve = gated * pre * bend
    grad_pre = gated * squash + curve
    bias_ref[0] = jnp.sum(grad_pre, axis=1, keepdims=True)
    gthr_ref[0] = -jnp.sum(curve, axis=1, keepdims=True)
    out_ref[0] = jnp.dot(
        grad_pre.astype(jnp.bfloat16), x_ref[0], preferred_element_type=jnp.float32
    ).astype(jnp.bfloat16)


def grad_enc(back, pre, thr, mask, whole):
    layers, features, count = pre.shape
    width = whole.shape[2]
    tile = min(512, features)
    column = pl.BlockSpec((1, tile, 1), lambda l, t: (l, t, 0))
    turned = pl.BlockSpec((1, tile, count), lambda l, t: (l, t, 0))
    return pl.pallas_call(
        grad_enc_kernel,
        grid=(layers, features // tile),
        out_shape=(
            jax.ShapeDtypeStruct((layers, features, width), jnp.bfloat16),
            jax.ShapeDtypeStruct((layers, features, 1), jnp.float32),
            jax.ShapeDtypeStruct((layers, features, 1), jnp.float32),
        ),
        in_specs=[
            turned,
            turned,
            column,
            pl.BlockSpec((1, 1, tile // BLOCK, count), lambda l, t: (l, t, 0, 0)),
            pl.BlockSpec((1, count, width), lambda l, t: (l, 0, 0)),
        ],
        out_specs=(pl.BlockSpec((1, tile, width), lambda l, t: (l, t, 0)), column, column),
        compiler_params=pltpu.CompilerParams(vmem_limit_bytes=40 * MIB),
        name="grad_enc",
    )(back, pre, thr, mask, whole)


def per_device(n_feat, n_layer, inputs, targets, block_mask, enc_weight, enc_bias, threshold, dec_weight):
    layers, features, width = enc_weight.shape
    place = lax.axis_index("layer")
    rows = inputs.shape[1]
    count = block_mask.shape[2]
    tile = min(512, features)
    blocks = features // BLOCK
    mask = lax.dynamic_slice_in_dim(block_mask, place * blocks, blocks, 1).astype(jnp.float32)
    mask = mask.reshape(layers, features // tile, tile // BLOCK, count)
    bias, thr = enc_bias[:, :, None], threshold[:, :, None]
    stages = n_layer.bit_length() - 1
    mine = bases(bits(place, stages), n_layer)[stages]
    tgt = targets.reshape(rows, layers, width // (n_layer * LANES), n_layer, LANES)
    tgt = lax.dynamic_index_in_dim(tgt, mine, 3, keepdims=False).transpose(1, 2, 0, 3)

    whole = gather(inputs, n_feat, n_layer)
    pre, turned, hidden = encode(whole, enc_weight, bias, thr, mask)
    err, back = exchange(hidden, dec_weight, tgt, n_feat, n_layer)
    dec_grads = grad_dec(turned, err, dec_weight.shape[0], width)
    enc_grads, grad_bias, grad_thr = grad_enc(back, pre, thr, mask, whole)
    return (
        enc_grads,
        grad_bias.reshape(layers, features),
        grad_thr.reshape(layers, features),
        dec_grads,
    )


def solution(mesh):
    return jax.shard_map(
        functools.partial(per_device, mesh.shape["feat"], mesh.shape["layer"]),
        mesh=mesh,
        in_specs=(
            P(None, ("groups", "feat"), None),
            P(("groups", "feat"), None, None),
            P(None, "feat", "groups"),
            P(None, ("feat", "layer"), None),
            P(None, ("feat", "layer")),
            P(None, ("feat", "layer")),
            P(None, ("feat", "layer"), None),
        ),
        out_specs=(
            P("groups", ("feat", "layer"), None),
            P("groups", ("feat", "layer")),
            P("groups", ("feat", "layer")),
            P("groups", ("feat", "layer"), None),
        ),
        check_vma=False,
    )
```

```python
import functools

import jax
import jax.numpy as jnp
from jax import lax
from jax.experimental import pallas as pl
from jax.experimental.pallas import tpu as pltpu
from jax.sharding import PartitionSpec as P

BLOCK = 128
BAND = 0.2
LANES = 128
MESH = pl.DeviceIdType.MESH
MIB = 1 << 20


def bits(index, stages):
    return [(index // (1 << j)) % 2 for j in range(stages)]


def bases(index_bits, count):
    out = [0]
    for j, bit in enumerate(index_bits):
        out.append(out[-1] + bit * (count >> (j + 1)))
    return out


def partners(index, index_bits):
    return [index + (1 - 2 * bit) * (1 << j) for j, bit in enumerate(index_bits)]


def greet(n_feat, feat, mates):
    barrier = pltpu.get_barrier_semaphore()
    for mate in mates:
        pl.semaphore_signal(barrier, inc=1, device_id={"layer": mate}, device_id_type=MESH)

    def one(o, carry):
        pl.semaphore_signal(
            barrier, inc=1, device_id={"feat": (feat + o) % n_feat}, device_id_type=MESH
        )
        return carry

    lax.fori_loop(1, n_feat, one, 0)
    pl.semaphore_wait(barrier, len(mates) + n_feat - 1)


def remote(src, dst, send, recv, where):
    return pltpu.make_async_remote_copy(
        src_ref=src, dst_ref=dst, send_sem=send, recv_sem=recv, device_id=where, device_id_type=MESH
    )


def gather_kernel(n_feat, n_layer, x_ref, out_ref, z_send, z_recv, l_send, l_recv, own_sem):
    feat, place = lax.axis_index("feat"), lax.axis_index("layer")
    stages = n_layer.bit_length() - 1
    rows = x_ref.shape[1]
    width = x_ref.shape[2] // n_layer
    place_bits = bits(place, stages)
    base = bases(place_bits, n_layer)
    mates = partners(place, place_bits)
    greet(n_feat, feat, mates)

    layers = x_ref.shape[0]
    pieces = (n_feat - 1) * layers

    def at(ref, l, source, first, count):
        return ref.at[
            l,
            pl.ds(pl.multiple_of(source * rows, rows), rows),
            pl.ds(pl.multiple_of(first * width, width), count * width),
        ]

    def z_copy(i):
        o, l = i // layers + 1, i % layers
        mine = at(out_ref, l, feat, base[stages], 1)
        src = x_ref.at[l, :, pl.ds(pl.multiple_of(base[stages] * width, width), width)]
        return remote(src, mine, z_send.at[i], z_recv.at[i], {"feat": (feat + o) % n_feat})

    def l_copy(j, i):
        o, l = i // layers + 1, i % layers
        part = at(out_ref, l, (feat + n_feat - o) % n_feat, base[j + 1], n_layer >> (j + 1))
        return remote(part, part, l_send.at[j, i], l_recv.at[j, i], {"layer": mates[j]})

    def start_z(o, carry):
        z_copy(o).start()
        return carry

    lax.fori_loop(0, pieces, start_z, 0)
    own = pltpu.make_async_copy(
        x_ref, out_ref.at[:, pl.ds(pl.multiple_of(feat * rows, rows), rows), :], own_sem
    )
    own.start()
    for j in reversed(range(-1, stages)):

        def hop(o, carry, j=j):
            if j == stages - 1:
                z_copy(o).wait_recv()
            else:
                l_copy(j + 1, o).wait_recv()
            if j >= 0:
                l_copy(j, o).start()
            return carry

        lax.fori_loop(0, pieces, hop, 0)

    def drain(o, carry):
        z_copy(o).wait_send()
        for j in range(stages):
            l_copy(j, o).wait_send()
        return carry

    lax.fori_loop(0, pieces, drain, 0)
    own.wait()


def gather(inputs, n_feat, n_layer):
    layers, rows, width = inputs.shape
    stages = n_layer.bit_length() - 1
    return pl.pallas_call(
        functools.partial(gather_kernel, n_feat, n_layer),
        out_shape=jax.ShapeDtypeStruct((layers, rows * n_feat, width), inputs.dtype),
        in_specs=[pl.BlockSpec(memory_space=pltpu.VMEM)],
        out_specs=pl.BlockSpec(memory_space=pltpu.VMEM),
        scratch_shapes=[
            pltpu.SemaphoreType.DMA(((n_feat - 1) * layers,)),
            pltpu.SemaphoreType.DMA(((n_feat - 1) * layers,)),
            pltpu.SemaphoreType.DMA((stages, (n_feat - 1) * layers)),
            pltpu.SemaphoreType.DMA((stages, (n_feat - 1) * layers)),
            pltpu.SemaphoreType.DMA,
        ],
        compiler_params=pltpu.CompilerParams(
            collective_id=0, has_side_effects=True, vmem_limit_bytes=60 * MIB
        ),
        name="gather_rows",
    )(inputs)


def column_of(ref, l, t, tile):
    row = ref[pl.ds(l, 1), pl.ds(pl.multiple_of(t * tile, tile), tile)]
    return jnp.broadcast_to(row, (LANES, tile)).T[:, :1]


def squash_of(pre, thr):
    return 0.5 + 0.5 * jnp.tanh((pre - thr) * (0.5 / BAND))


def row_of(column):
    return jnp.broadcast_to(column, (column.shape[0], LANES)).T[:1]


def gate_tile(mask_ref, l, t, values):
    mask = mask_ref[l, t]
    shape = (mask.shape[0], BLOCK, values.shape[1])
    return jnp.broadcast_to(mask[:, None, :], shape).reshape(values.shape)


def encode_kernel(x_ref, w_ref, bias_ref, thr_ref, mask_ref, pre_ref, turned_ref, hidden_ref):
    l, t = pl.program_id(0), pl.program_id(1)
    tile = w_ref.shape[1]
    pre = lax.dot_general(
        w_ref[0], x_ref[0], (((1,), (1,)), ((), ())), preferred_element_type=jnp.float32
    ) + column_of(bias_ref, l, t, tile)
    squash = squash_of(pre, column_of(thr_ref, l, t, tile))
    hidden = (gate_tile(mask_ref, l, t, pre) * pre * squash).astype(jnp.bfloat16)
    pre_ref[0] = pre
    turned_ref[0] = hidden
    hidden_ref[0] = hidden.T


def encode(whole, enc_weight, bias, thr, mask):
    layers, count, width = whole.shape
    features = enc_weight.shape[1]
    tile = min(1024, features)
    row = pl.BlockSpec((layers, features), lambda l, t: (0, 0))
    turned = pl.BlockSpec((1, tile, count), lambda l, t: (l, t, 0))
    return pl.pallas_call(
        encode_kernel,
        grid=(layers, features // tile),
        out_shape=(
            jax.ShapeDtypeStruct((layers, features, count), jnp.float32),
            jax.ShapeDtypeStruct((layers, features, count), jnp.bfloat16),
            jax.ShapeDtypeStruct((layers, count, features), jnp.bfloat16),
        ),
        in_specs=[
            pl.BlockSpec((1, count, width), lambda l, t: (l, 0, 0)),
            pl.BlockSpec((1, tile, width), lambda l, t: (l, t, 0)),
            row,
            row,
            pl.BlockSpec(mask.shape, lambda l, t: (0, 0, 0, 0)),
        ],
        out_specs=(turned, turned, pl.BlockSpec((1, count, tile), lambda l, t: (l, 0, t))),
        compiler_params=pltpu.CompilerParams(vmem_limit_bytes=60 * MIB),
        name="encode",
    )(whole, enc_weight, bias, thr, mask)


def exchange_kernel(
    n_feat, n_layer, hidden_ref, w_hbm, tgt_ref, err_ref, back_ref,
    wbuf, dec, z_got, w_sem, z_send, z_recv, g_send, g_recv, r_send, r_recv, a_send, a_recv, *got,
):
    feat, place = lax.axis_index("feat"), lax.axis_index("layer")
    stages = n_layer.bit_length() - 1
    layers, count, features = hidden_ref.shape
    rows = count // n_feat
    chunks = dec.shape[0]
    cols = n_layer * LANES
    splits = chunks // layers
    pairs = wbuf.shape[0]
    place_bits = bits(place, stages)
    base = bases(place_bits, n_layer)
    mates = partners(place, place_bits)
    mine = base[stages]
    held = [n_layer >> (j + 1) for j in range(stages)]

    def load(p, n):
        part = w_hbm.at[p, :, pl.ds(n * cols, cols)]
        return pltpu.make_async_copy(part, wbuf.at[p, n], w_sem.at[p, n])

    for n in range(splits):
        for p in range(pairs):
            load(p, n).start()
    greet(n_feat, feat, mates)

    tile = min(512, features)

    @pl.loop(0, layers * (features // tile))
    def _(i):
        l, t = i // (features // tile), i % (features // tile)
        back_ref[l, pl.ds(pl.multiple_of(t * tile, tile), tile), :] = jnp.zeros(
            (tile, count), jnp.float32
        )

    def reduce_copy(j, k):
        away = base[j] + (1 - place_bits[j]) * held[j]
        return remote(
            dec.at[k, pl.ds(away, held[j])], got[j].at[k],
            r_send.at[j, k], r_recv.at[j, k], {"layer": mates[j]},
        )

    def spread_copy(j, k):
        part = err_ref.at[k, pl.ds(base[j + 1], held[j])]
        return remote(part, part, a_send.at[j, k], a_recv.at[j, k], {"layer": mates[j]})

    def own_rows(which):
        return pl.ds(pl.multiple_of(which * rows, rows), rows)

    def all_bytes(k, sem):
        return pltpu.make_async_copy(z_got.at[k], z_got.at[k], sem)

    def decode(k):
        m, n = k % layers, k // layers
        wide = min(2, n_layer)

        def run(sources):
            for p in sources:
                load(p, n).wait()

            @pl.loop(0, n_layer // wide)
            def _(c):
                lanes = pl.ds(pl.multiple_of(c * wide * LANES, wide * LANES), wide * LANES)
                total = None
                for p, l in sources.items():
                    term = jnp.dot(
                        hidden_ref[l], wbuf[p, n, :, lanes], preferred_element_type=jnp.float32
                    )
                    total = term if total is None else total + term
                total = total.astype(jnp.bfloat16)
                for i in range(wide):
                    dec[k, c * wide + i] = total[:, i * LANES : (i + 1) * LANES]

        pl.when(m == 0)(lambda: run({0: 0}))
        pl.when(m == 1)(lambda: run({1: 0, 2: 1}))
        reduce_copy(0, k).start()

    def fold(j, k):
        reduce_copy(j, k).wait_recv()
        part = pl.ds(base[j + 1], held[j])
        total = dec[k, part].astype(jnp.float32) + got[j][k].astype(jnp.float32)
        dec[k, part] = total.astype(jnp.bfloat16)
        if j + 1 < stages:
            reduce_copy(j + 1, k).start()
        else:

            def send(o, carry):
                there = (feat + o) % n_feat
                remote(
                    dec.at[k, mine, own_rows(there)], z_got.at[k, o - 1],
                    z_send.at[k], z_recv.at[k], {"feat": there},
                ).start()
                return carry

            lax.fori_loop(1, n_feat, send, 0)

    def finish(k):
        all_bytes(k, z_recv.at[k]).wait()
        m, n = k % layers, k // layers
        total = dec[k, mine, own_rows(feat)].astype(jnp.float32)
        total = total + jnp.sum(z_got[k].astype(jnp.float32), axis=0)
        error = total - tgt_ref[m, n].astype(jnp.float32)
        part = err_ref.at[k, mine, own_rows(feat)]
        part[...] = error.astype(jnp.bfloat16)

        def send(o, carry):
            there = (feat + o) % n_feat
            remote(part, part, g_send.at[k], g_recv.at[k], {"feat": there}).start()
            return carry

        lax.fori_loop(1, n_feat, send, 0)

    def spread(j, k):
        if j == stages - 1:
            all_bytes(k, g_recv.at[k]).wait()
        else:
            spread_copy(j + 1, k).wait_recv()
        spread_copy(j, k).start()

    def pull(k):
        spread_copy(0, k).wait_recv()
        m, n = k % layers, k // layers

        def run(sources):
            error = jnp.concatenate([err_ref[k, b] for b in range(n_layer)], axis=1)
            for p, l in sources.items():

                @pl.loop(0, features // tile)
                def _(t, p=p, l=l):
                    part = pl.ds(pl.multiple_of(t * tile, tile), tile)
                    back_ref[l, part, :] += lax.dot_general(
                        wbuf[p, n, part, :], error, (((1,), (1,)), ((), ())),
                        preferred_element_type=jnp.float32,
                    )

        pl.when(m == 0)(lambda: run({0: 0}))
        pl.when(m == 1)(lambda: run({1: 0, 2: 1}))

    steps = [decode]
    steps += [functools.partial(fold, j) for j in range(stages)]
    steps += [finish]
    steps += [functools.partial(spread, j) for j in reversed(range(stages))]
    steps += [pull]

    @pl.loop(0, chunks + len(steps) - 1)
    def _(s):
        for late in reversed(range(1, len(steps) - 1)):
            k = s - late
            pl.when((k >= 0) & (k < chunks))(functools.partial(steps[late], k))
        pl.when(s < chunks)(functools.partial(decode, s))
        k = s - (len(steps) - 1)
        pl.when(k >= 0)(functools.partial(pull, k))

    @pl.loop(0, chunks)
    def _(k):
        all_bytes(k, z_send.at[k]).wait()
        all_bytes(k, g_send.at[k]).wait()
        for j in range(stages):
            reduce_copy(j, k).wait_send()
            spread_copy(j, k).wait_send()


def exchange(hidden, dec_weight, tgt, n_feat, n_layer):
    layers, count, features = hidden.shape
    pairs, _, width = dec_weight.shape
    stages = n_layer.bit_length() - 1
    splits = width // (n_layer * LANES)
    chunks = splits * layers
    rows = count // n_feat
    dma = pltpu.SemaphoreType.DMA
    vmem = pl.BlockSpec(memory_space=pltpu.VMEM)
    return pl.pallas_call(
        functools.partial(exchange_kernel, n_feat, n_layer),
        out_shape=(
            jax.ShapeDtypeStruct((chunks, n_layer, count, LANES), jnp.bfloat16),
            jax.ShapeDtypeStruct((layers, features, count), jnp.float32),
        ),
        in_specs=[vmem, pl.BlockSpec(memory_space=pl.ANY), vmem],
        out_specs=(vmem, vmem),
        scratch_shapes=[
            pltpu.VMEM((pairs, splits, features, n_layer * LANES), jnp.bfloat16),
            pltpu.VMEM((chunks, n_layer, count, LANES), jnp.bfloat16),
            pltpu.VMEM((chunks, n_feat - 1, rows, LANES), jnp.bfloat16),
            dma((pairs, splits)),
            dma((chunks,)),
            dma((chunks,)),
            dma((chunks,)),
            dma((chunks,)),
            dma((stages, chunks)),
            dma((stages, chunks)),
            dma((stages, chunks)),
            dma((stages, chunks)),
        ]
        + [
            pltpu.VMEM((chunks, n_layer >> (j + 1), count, LANES), jnp.bfloat16)
            for j in range(stages)
        ],
        compiler_params=pltpu.CompilerParams(
            collective_id=1, has_side_effects=True, vmem_limit_bytes=60 * MIB
        ),
        name="decode_exchange",
    )(hidden, dec_weight, tgt)


def grad_dec_kernel(layers, turned_ref, err_ref, out_ref):
    goal = (pl.program_id(0) + 1) // 2
    n_layer = err_ref.shape[1]
    cols = n_layer * LANES
    for n in range(err_ref.shape[0] // layers):
        error = jnp.concatenate([err_ref[n * layers + goal, b] for b in range(n_layer)], axis=1)
        out_ref[0, :, n * cols : (n + 1) * cols] = jnp.dot(
            turned_ref[0], error, preferred_element_type=jnp.float32
        ).astype(jnp.bfloat16)


def grad_dec(turned, err, pairs, width):
    layers, features, count = turned.shape
    tile = min(1024, features)
    return pl.pallas_call(
        functools.partial(grad_dec_kernel, layers),
        grid=(pairs, features // tile),
        out_shape=jax.ShapeDtypeStruct((pairs, features, width), jnp.bfloat16),
        in_specs=[
            pl.BlockSpec((1, tile, count), lambda p, t: (p // 2, t, 0)),
            pl.BlockSpec(err.shape, lambda p, t: (0, 0, 0, 0)),
        ],
        out_specs=pl.BlockSpec((1, tile, width), lambda p, t: (p, t, 0)),
        compiler_params=pltpu.CompilerParams(vmem_limit_bytes=60 * MIB),
        name="grad_dec",
    )(turned, err)


def grad_enc_kernel(back_ref, pre_ref, thr_ref, mask_ref, x_ref, out_ref, bias_ref, gthr_ref):
    l, t = pl.program_id(0), pl.program_id(1)
    pre = pre_ref[0]
    back = back_ref[0]
    tile = pre.shape[0]
    squash = squash_of(pre, column_of(thr_ref, l, t, tile))
    bend = squash * (1.0 - squash) * (1.0 / BAND)
    gated = back * gate_tile(mask_ref, l, t, pre)
    curve = gated * pre * bend
    grad_pre = gated * squash + curve
    place = (pl.ds(l, 1), pl.ds(pl.multiple_of(t * tile, tile), tile))
    bias_ref[place] = row_of(jnp.sum(grad_pre, axis=1, keepdims=True))
    gthr_ref[place] = row_of(-jnp.sum(curve, axis=1, keepdims=True))
    out_ref[0] = jnp.dot(
        grad_pre.astype(jnp.bfloat16), x_ref[0], preferred_element_type=jnp.float32
    ).astype(jnp.bfloat16)


def grad_enc(back, pre, thr, mask, whole):
    layers, features, count = pre.shape
    width = whole.shape[2]
    tile = min(1024, features)
    row = pl.BlockSpec((layers, features), lambda l, t: (0, 0))
    turned = pl.BlockSpec((1, tile, count), lambda l, t: (l, t, 0))
    return pl.pallas_call(
        grad_enc_kernel,
        grid=(layers, features // tile),
        out_shape=(
            jax.ShapeDtypeStruct((layers, features, width), jnp.bfloat16),
            jax.ShapeDtypeStruct((layers, features), jnp.float32),
            jax.ShapeDtypeStruct((layers, features), jnp.float32),
        ),
        in_specs=[
            turned,
            turned,
            row,
            pl.BlockSpec(mask.shape, lambda l, t: (0, 0, 0, 0)),
            pl.BlockSpec((1, count, width), lambda l, t: (l, 0, 0)),
        ],
        out_specs=(pl.BlockSpec((1, tile, width), lambda l, t: (l, t, 0)), row, row),
        compiler_params=pltpu.CompilerParams(vmem_limit_bytes=60 * MIB),
        name="grad_enc",
    )(back, pre, thr, mask, whole)


def per_device(n_feat, n_layer, inputs, targets, block_mask, enc_weight, enc_bias, threshold, dec_weight):
    layers, features, width = enc_weight.shape
    place = lax.axis_index("layer")
    rows = inputs.shape[1]
    count = block_mask.shape[2]
    tile = min(1024, features)
    blocks = features // BLOCK
    mask = lax.dynamic_slice_in_dim(block_mask, place * blocks, blocks, 1).astype(jnp.float32)
    mask = mask.reshape(layers, features // tile, tile // BLOCK, count)
    stages = n_layer.bit_length() - 1
    mine = bases(bits(place, stages), n_layer)[stages]
    tgt = targets.reshape(rows, layers, width // (n_layer * LANES), n_layer, LANES)
    tgt = lax.dynamic_index_in_dim(tgt, mine, 3, keepdims=False).transpose(1, 2, 0, 3)

    whole = gather(inputs, n_feat, n_layer)
    pre, turned, hidden = encode(whole, enc_weight, enc_bias, threshold, mask)
    err, back = exchange(hidden, dec_weight, tgt, n_feat, n_layer)
    dec_grads = grad_dec(turned, err, dec_weight.shape[0], width)
    enc_grads, grad_bias, grad_thr = grad_enc(back, pre, threshold, mask, whole)
    return enc_grads, grad_bias, grad_thr, dec_grads


def solution(mesh):
    return jax.shard_map(
        functools.partial(per_device, mesh.shape["feat"], mesh.shape["layer"]),
        mesh=mesh,
        in_specs=(
            P(None, ("groups", "feat"), None),
            P(("groups", "feat"), None, None),
            P(None, "feat", "groups"),
            P(None, ("feat", "layer"), None),
            P(None, ("feat", "layer")),
            P(None, ("feat", "layer")),
            P(None, ("feat", "layer"), None),
        ),
        out_specs=(
            P("groups", ("feat", "layer"), None),
            P("groups", ("feat", "layer")),
            P("groups", ("feat", "layer")),
            P("groups", ("feat", "layer"), None),
        ),
        check_vma=False,
    )
```
